128 devices in a mesh: dc: 16 (over z, x_lo, core), tp: 8 (over y, x_hi).
Axes of the slice: x: 4 (x_hi: 2, x_lo: 2; x = x_hi * 2 + x_lo), y: 4, z: 4, core: 2. Of those that a mesh axis runs over, the one named last changes fastest.
Arguments:
- query_heads: bfloat16 [3584, 8192], P('dc', 'tp'), may hold values from -10 to 10
- key_heads: bfloat16 [3584, 1024], P('dc', 'tp'), may hold values from -11 to 11
- value_heads: bfloat16 [3584, 1024], P('dc', 'tp'), may hold values from -6 to 6
- out_weight: bfloat16 [8192, 8192], P('tp'), may hold values from -0.0625 to 0.0625
- grad_out: bfloat16 [3584, 8192], P('dc', 'tp'), may hold values from -6 to 6
- span_place: int32 [32], replicated, may hold values from 0 to 31, each once
- sample_lengths: int32 [4], replicated, may hold values from 1 to 1792, 3584 in all
Outputs:
- layer_out: bfloat16 [3584, 8192], P('dc', 'tp')
- grad_queries: bfloat16 [3584, 8192], P('dc', 'tp')
- grad_keys: bfloat16 [3584, 1024], P('dc', 'tp')
- grad_values: bfloat16 [3584, 1024], P('dc', 'tp')
- grad_weight: bfloat16 [8192, 8192], P('tp', 'dc')
The draws below stay inside these ranges and needn't reach their ends.
Inputs may be any that keep to these rules, and one draw needn't show every extreme that they name: `span_place`: each of 0 to 31 once. `sample_lengths`: the lengths sum to 3584; the longest is exactly 1792.
All inputs are finite; a program needn't handle non-finite values.
Results may differ from the reference program's by a relative error of at most 0.039.
Values may be sent and summed in bfloat16 or wider, within the bound.
A program may use at most 128 MiB of HBM per device.

```python
import math
import jax
import jax.numpy as jnp
import numpy as np
from jax import lax

D = 8192
HEADS = 64
KV_HEADS = 8
HEAD_DIM = 128
TOK_DEV = 224
SAMPLES = 4
TOKENS = 3584
SPANS = 32
N_DC = 16
N_TP = 8


def draw_query_heads(key, part):
    key = jax.random.fold_in(key, 5)
    shape_four = (TOKENS, KV_HEADS, HEADS // KV_HEADS, HEAD_DIM)
    drawn = jnp.clip(jax.random.normal(key, shape_four, jnp.float32), -6.0, 6.0)
    return drawn.reshape(TOKENS, HEADS * HEAD_DIM).astype(jnp.bfloat16)


def draw_key_heads(key, part):
    key = jax.random.fold_in(key, 7)
    shape_three = (TOKENS, KV_HEADS, HEAD_DIM)
    drawn = jnp.clip(jax.random.normal(key, shape_three, jnp.float32), -6.0, 6.0)
    return drawn.reshape(TOKENS, KV_HEADS * HEAD_DIM).astype(jnp.bfloat16)


def raised(array, rng, source, target, parts, factor):
    owner, partner = [(jnp.arange(array.shape[position]) // (array.shape[position] // parts)).reshape([-1 if axis == position else 1 for axis in range(array.ndim)]) for position in (source, target)]
    chosen = jax.random.permutation(rng, parts)[partner]
    strong = (owner == chosen) | (owner == (partner + parts // 2) % parts)
    return jnp.where(strong, factor * array, array)


def block_levels(key, extent, shards, low, largest):
    factor_of = 1.0
    for dim, shards_of in shards:
        heights = jax.random.uniform(jax.random.fold_in(jax.random.fold_in(key, 6), dim), (shards_of,), jnp.float32, low / len(shards), largest / len(shards))
        factor_of = factor_of * jnp.repeat(jnp.exp(heights), extent[dim] // shards_of).reshape((-1,) + (1,) * (len(extent) - 1 - dim))
    return factor_of


def profile(amount, total, bound, skew):
    portions = [(1 << 20) // math.isqrt(grade ** skew) + 1 for grade in range(2, amount + 1)]
    spare, holding = total - bound - (amount - 1), [1] * (amount - 1)
    while spare > 0:
        candidates = [i for i in range(amount - 1) if holding[i] < bound]
        pool, remaining = sum([portions[i] for i in candidates]), spare
        for i in candidates:
            addition = min(bound - holding[i], max(1, remaining * portions[i] // pool), spare)
            holding[i] = holding[i] + addition
            spare = spare - addition
    return np.array([bound] + holding)


def uneven_parts(rng, amount, total, reach, lean):
    if amount == 2:
        one = jax.random.randint(rng, (), max(1, total - reach), min(reach, total - 1) + 1)
        return jnp.stack([one, total - one])
    lengths = jnp.asarray(profile(amount, total, reach, lean), jnp.int32)
    pairs = (amount - 1) // 2
    donor, taker = lengths[1:1 + 2 * pairs:2], lengths[2:2 + 2 * pairs:2]
    room = jnp.minimum(donor - 1, reach - taker)
    shifted = jax.random.randint(jax.random.fold_in(rng, 1), (pairs,), 0, 1 << 20) % (room + 1)
    lengths = lengths.at[1:1 + 2 * pairs:2].set(donor - shifted).at[2:2 + 2 * pairs:2].set(taker + shifted)
    return lengths[jax.random.permutation(jax.random.fold_in(rng, 2), amount)]


def noise(own_key, dims, spread, reach, pieces=(), kind=jnp.bfloat16):
    result = spread * jax.random.normal(own_key, dims, jnp.float32)
    if pieces:
        result = result * block_levels(own_key, dims, pieces, -0.22, 0.18)
    return jnp.clip(result, -reach, reach).astype(kind)


def heavy_noise(own_key, dims, spread, bound, pieces, heavy, kind=jnp.bfloat16):
    array = spread * jax.random.normal(own_key, dims, jnp.float32)
    if pieces:
        array = array * block_levels(own_key, dims, pieces, -0.22, 0.18)
    return jnp.clip(raised(array, jax.random.fold_in(own_key, 3), *heavy), -bound, bound).astype(kind)


def setup_inputs(seed: int = 0) -> dict:
    streams_of = jax.random.split(jax.random.key(seed), 8)
    return {
        "query_heads": draw_query_heads(jax.random.fold_in(streams_of[7], 71), 0),
        "key_heads": draw_key_heads(jax.random.fold_in(streams_of[7], 71), 0),
        "value_heads": noise(streams_of[2], (TOKENS, KV_HEADS * HEAD_DIM), 1.0, 6.0, ((0, 16), (1, 8))),
        "out_weight": noise(streams_of[3], (HEADS * HEAD_DIM, D), (HEADS * HEAD_DIM) ** -0.5, 0.0625, ((0, 8),)),
        "grad_out": heavy_noise(streams_of[4], (TOKENS, D), 1.0, 6.0, ((0, 16), (1, 8)), (0, 1, 16, 2.0)),
        "span_place": jax.random.permutation(streams_of[5], SPANS).astype(jnp.int32),
        "sample_lengths": uneven_parts(streams_of[6], SAMPLES, TOKENS, TOKENS // 2, 2).astype(jnp.int32),
    }


negative_fill = -1.0e30


def token_positions(span_place, total_rows, span_count):
    span_rows = total_rows // span_count
    indices = jnp.arange(total_rows, dtype=jnp.int32)
    matches = (indices // span_rows)[:, None] == jnp.arange(span_count, dtype=jnp.int32)[None, :]
    placed = jnp.sum(jnp.where(matches, span_place[None, :], 0), axis=1).astype(jnp.int32)
    return placed * span_rows + indices % span_rows


def sample_ids(positions, sample_lengths):
    bounds = jnp.cumsum(sample_lengths).astype(jnp.int32)
    return jnp.sum((positions[:, None] >= bounds[None, :]).astype(jnp.int32), axis=1)


def head_block(queries, keys_group, values_group, grads, query_pos, query_sample, key_pos, key_sample):
    scaling = HEAD_DIM ** -0.5
    allowed = (key_sample[None, :] == query_sample[:, None]) & (key_pos[None, :] <= query_pos[:, None])
    scores = jnp.einsum("trd,nd->rtn", queries.astype(jnp.float32), keys_group.astype(jnp.float32)) * scaling
    scores = jnp.where(allowed[None], scores, negative_fill)
    highest = jnp.max(scores, axis=-1, keepdims=True)
    expo = jnp.where(allowed[None], jnp.exp(scores - highest), 0.0)
    totals = jnp.sum(expo, axis=-1, keepdims=True)
    probs = expo / totals
    weights = probs.astype(jnp.bfloat16)
    attended = jnp.einsum("rtn,nd->trd", weights.astype(jnp.float32), values_group.astype(jnp.float32)).astype(jnp.bfloat16)
    dprob = jnp.einsum("trd,nd->rtn", grads.astype(jnp.float32), values_group.astype(jnp.float32))
    delta = jnp.sum(grads.astype(jnp.float32) * attended.astype(jnp.float32), axis=-1).T
    dscore = (probs * (dprob - delta[:, :, None])).astype(jnp.bfloat16)
    grad_q = jnp.einsum("rtn,nd->trd", dscore.astype(jnp.float32), keys_group.astype(jnp.float32)) * scaling
    grad_k = jnp.einsum("rtn,trd->nd", dscore.astype(jnp.float32), queries.astype(jnp.float32)) * scaling
    grad_v = jnp.einsum("rtn,trd->nd", weights.astype(jnp.float32), grads.astype(jnp.float32))
    return attended, grad_q, grad_k, grad_v


def reference(query_heads, key_heads, value_heads, out_weight, grad_out, span_place, sample_lengths):
    positions = token_positions(span_place, TOKENS, SPANS)
    samples = sample_ids(positions, sample_lengths)
    repeats = HEADS // KV_HEADS
    head_cols = HEADS * HEAD_DIM
    head_grads = jnp.dot(grad_out, out_weight.T, preferred_element_type=jnp.float32).astype(jnp.bfloat16)
    query_five = query_heads.reshape(N_DC, TOK_DEV, KV_HEADS, repeats, HEAD_DIM).transpose(2, 0, 1, 3, 4)
    grad_five = head_grads.reshape(N_DC, TOK_DEV, KV_HEADS, repeats, HEAD_DIM).transpose(2, 0, 1, 3, 4)
    keys_grouped = key_heads.reshape(TOKENS, KV_HEADS, HEAD_DIM).transpose(1, 0, 2)
    values_grouped = value_heads.reshape(TOKENS, KV_HEADS, HEAD_DIM).transpose(1, 0, 2)
    query_pos = positions.reshape(N_DC, TOK_DEV)
    query_samples = samples.reshape(N_DC, TOK_DEV)

    def per_group(operands):
        group_queries, group_grads, group_keys, group_values = operands

        def per_rows(carry, rows):
            queries_rows, grads_rows, pos_rows, sample_rows = rows
            attended, grad_q, grad_k, grad_v = head_block(queries_rows, group_keys, group_values, grads_rows, pos_rows, sample_rows, positions, samples)
            return (carry[0] + grad_k, carry[1] + grad_v), (attended, grad_q)

        start_sums = (jnp.zeros((TOKENS, HEAD_DIM), jnp.float32), jnp.zeros((TOKENS, HEAD_DIM), jnp.float32))
        sums, results = lax.scan(per_rows, start_sums, (group_queries, group_grads, query_pos, query_samples))
        return results[0], results[1], sums[0], sums[1]

    attended, grad_q, grad_k, grad_v = lax.map(per_group, (query_five, grad_five, keys_grouped, values_grouped))
    attended = attended.transpose(1, 2, 0, 3, 4).reshape(TOKENS, head_cols)
    grad_queries = grad_q.transpose(1, 2, 0, 3, 4).reshape(TOKENS, head_cols).astype(jnp.bfloat16)
    grad_keys = grad_k.transpose(1, 0, 2).reshape(TOKENS, KV_HEADS * HEAD_DIM).astype(jnp.bfloat16)
    grad_values = grad_v.transpose(1, 0, 2).reshape(TOKENS, KV_HEADS * HEAD_DIM).astype(jnp.bfloat16)
    cols_dev = head_cols // N_TP
    layer_sum = jnp.zeros((TOKENS, D), jnp.float32)
    for member in range(N_TP):
        partial_out = jnp.dot(attended[:, member * cols_dev:(member + 1) * cols_dev], out_weight[member * cols_dev:(member + 1) * cols_dev], preferred_element_type=jnp.float32).astype(jnp.bfloat16)
        layer_sum = layer_sum + lax.optimization_barrier(partial_out).astype(jnp.float32)
    layer_out = layer_sum.astype(jnp.bfloat16)

    def add_partial(running, rows):
        attended_rows, grad_rows = rows
        partial_grad = jnp.dot(attended_rows.T, grad_rows, preferred_element_type=jnp.float32).astype(jnp.bfloat16)
        return running + lax.optimization_barrier(partial_grad).astype(jnp.float32), None

    weight_sum, unused = lax.scan(add_partial, jnp.zeros((head_cols, D), jnp.float32), (attended.reshape(N_DC, TOK_DEV, head_cols), grad_out.reshape(N_DC, TOK_DEV, D)))
    grad_weight = weight_sum.astype(jnp.bfloat16)
    return (layer_out, grad_queries, grad_keys, grad_values, grad_weight)
```

```python
import functools

import jax
import jax.numpy as jnp
from jax import lax
from jax.experimental import pallas as pl
from jax.experimental.pallas import tpu as pltpu
from jax.sharding import PartitionSpec as P

HEAD_DIM = 128
ROWS = 224
SPAN = 112
GROUP = 8
ZK = 896
COLS = 1024
HALF = 112
SCALE = HEAD_DIM**-0.5
SCALE2 = SCALE * 1.4426950408889634
FILL = -1e30
MESH = pl.DeviceIdType.MESH
F32 = jnp.float32
BF16 = jnp.bfloat16


def dot_nn(a, b):
    return lax.dot_general(a, b, (((1,), (0,)), ((), ())), preferred_element_type=F32)


def dot_nt(a, b):
    return lax.dot_general(a, b, (((1,), (1,)), ((), ())), preferred_element_type=F32)


def dot_tn(a, b):
    return lax.dot_general(a, b, (((0,), (0,)), ((), ())), preferred_element_type=F32)


class Here:
    def __init__(self):
        d = lax.axis_index("dc")
        t = lax.axis_index("tp")
        self.d, self.t = d, t
        self.c = lax.rem(d, 2)
        self.x = lax.rem(lax.div(d, 2), 2)
        self.z = lax.div(d, 4)
        self.h = lax.rem(t, 2)
        self.y = lax.div(t, 2)

    def by_dc(self, z, x):
        return ((z * 2 + x) * 2 + self.c, self.t)

    def by_tp(self, y, h):
        return (self.d, y * 2 + h)

    def sibling(self):
        return ((self.z * 2 + self.x) * 2 + (1 - self.c), self.t)


def around(a):
    return lax.rem(a + 1, 4), lax.rem(a + 3, 4), lax.rem(a + 2, 4)


def meet(devices):
    barrier = pltpu.get_barrier_semaphore()
    for device in devices:
        pl.semaphore_signal(barrier, inc=1, device_id=device, device_id_type=MESH)
    pl.semaphore_wait(barrier, len(devices))


class Gather:
    def __init__(self, view, a, b, dev, ssem, rsem):
        up, dn, far = around(a)
        o = 1 - b
        self.view, self.ssem, self.rsem = view, ssem, rsem
        self.out = [
            (a, b, None, dev(a, o)),
            (a, b, None, dev(up, b)),
            (a, b, None, dev(dn, b)),
            (a, o, None, dev(up, b)),
            (a, o, None, dev(dn, b)),
            (dn, b, 0, dev(up, b)),
            (up, b, 1, dev(dn, b)),
            (dn, o, 0, dev(up, b)),
            (up, o, 1, dev(dn, b)),
        ]
        self.into = [
            (a, o, None),
            (dn, b, None),
            (up, b, None),
            (dn, o, None),
            (up, o, None),
            (far, b, 0),
            (far, b, 1),
            (far, o, 0),
            (far, o, 1),
        ]

    def sent(self, i):
        a, b, half, device = self.out[i]
        ref = self.view(a, b, half)
        return pltpu.make_async_remote_copy(
            ref, ref, self.ssem.at[i], self.rsem.at[i], device_id=device, device_id_type=MESH
        )

    def got(self, i):
        a, b, half = self.into[i]
        ref = self.view(a, b, half)
        pltpu.make_async_remote_copy(
            ref, ref, self.ssem.at[i], self.rsem.at[i], device_id=self.out[i][3], device_id_type=MESH
        ).wait_recv()

    def start(self):
        for i in (1, 2, 0):
            self.sent(i).start()

    def pair(self):
        self.got(0)
        self.sent(3).start()
        self.sent(4).start()

    def near(self):
        self.got(1)
        self.sent(5).start()
        self.got(2)
        self.sent(6).start()

    def near_pair(self):
        self.got(3)
        self.sent(7).start()
        self.got(4)
        self.sent(8).start()

    def far(self):
        self.got(5)
        self.got(6)

    def far_pair(self):
        self.got(7)
        self.got(8)

    def drain(self):
        for i in range(9):
            self.sent(i).wait_send()


class Sibling:
    def __init__(self, view, here, ssem, rsem):
        up, dn, far = around(here.z)
        x, o = here.x, 1 - here.x
        self.here, self.view, self.ssem, self.rsem = here, view, ssem, rsem
        self.blocks = [
            (here.z, x), (here.z, o), (dn, x), (up, x), (dn, o), (up, o), (far, x), (far, o),
        ]

    def sent(self, i, core):
        z, x = self.blocks[i]
        ref = self.view(z, x, core)
        return pltpu.make_async_remote_copy(
            ref, ref, self.ssem.at[i], self.rsem.at[i],
            device_id=self.here.sibling(), device_id_type=MESH,
        )

    def start(self, *order):
        for i in order:
            self.sent(i, self.here.c).start()

    def got(self, *order):
        for i in order:
            self.sent(i, 1 - self.here.c).wait_recv()

    def drain(self):
        for i in range(8):
            self.sent(i, self.here.c).wait_send()


class Reduce:
    def __init__(self, emit, a, b, dev, sbuf, rbuf, ssem, rsem):
        up, dn, far = around(a)
        self.emit, self.b, self.sbuf, self.rbuf, self.ssem, self.rsem = emit, b, sbuf, rbuf, ssem, rsem
        u, d, p = dev(up, b), dev(dn, b), dev(a, 1 - b)
        self.devices = [u, d, u, d, u, d, p]

    def copy(self, i):
        return pltpu.make_async_remote_copy(
            self.sbuf.at[i], self.rbuf.at[i], self.ssem.at[i], self.rsem.at[i],
            device_id=self.devices[i], device_id_type=MESH,
        )

    def send(self, i, which, b, adds=()):
        self.emit(self.sbuf.at[i], which, b, [self.rbuf.at[j] for j in adds])
        self.copy(i).start()

    def far(self):
        self.send(0, "far", 0)
        self.send(1, "far", 1)

    def near(self):
        self.send(2, "up", 1)
        self.send(3, "dn", 0)

    def comb(self):
        self.copy(0).wait_recv()
        self.send(4, "up", 0, [0])
        self.copy(1).wait_recv()
        self.send(5, "dn", 1, [1])

    def pair(self):
        for i in (2, 3, 4, 5):
            self.copy(i).wait_recv()
        o = 1 - self.b
        self.send(6, "own", o, [4 + o, 3 - o])

    def final(self, out):
        self.copy(6).wait_recv()
        b = self.b
        self.emit(out, "own", b, [self.rbuf.at[j] for j in (4 + b, 3 - b, 6)])

    def drain(self):
        for i in range(7):
            self.copy(i).wait_send()


def write_bias(bias, place_ref, length_ref, here):
    row = lax.broadcasted_iota(jnp.int32, (ROWS, 1), 0)
    first, second = place_ref[2 * here.d], place_ref[2 * here.d + 1]
    pos = row + jnp.where(row < SPAN, first * SPAN, second * SPAN - SPAN)
    low = jnp.zeros((ROWS, 1), jnp.int32)
    bound = length_ref[0]
    for i in range(1, 4):
        low = jnp.where(pos >= bound, bound, low)
        bound = bound + length_ref[i]

    def fill(z, carry):
        lane = lax.broadcasted_iota(jnp.int32, (1, ZK), 1)
        key = jnp.zeros((1, ZK), jnp.int32)
        for i in range(8):
            begin = place_ref[8 * z + i] * SPAN - i * SPAN
            key = jnp.where(lane >= i * SPAN, lane + begin, key)
        bias[z] = jnp.where((key >= low) & (key <= pos), 0.0, FILL)
        return carry

    lax.fori_loop(0, 4, fill, 0)


def split_heads(dst, src):
    for head in range(GROUP):
        dst[head] = src[:, head * HEAD_DIM : (head + 1) * HEAD_DIM]


def keys_of(kv, which, z):
    return kv[which, pl.ds(4 * z, 4)].reshape(ZK, HEAD_DIM)


def forward_kernel(
    q_ref, k_ref, v_ref, w_ref, g_ref, place_ref, length_ref,
    att_ref, hg_ref, lse_ref, kv_out,
    kv, gbuf, wbuf, q_s, bias, top, total, oacc, hacc,
    wsem, kv_s, kv_r, sib_s, sib_r, g_s, g_r, out_sem,
):
    here = Here()

    def load_w(j):
        return pltpu.make_async_copy(w_ref.at[:, pl.ds(j * COLS, COLS)], wbuf.at[j], wsem.at[j])

    def kv_view(z, x, core, half=None):
        slot = (z * 2 + x) * 2 + core
        if half is None:
            return kv.at[:, slot]
        return kv.at[:, slot, pl.ds(half * HALF, HALF)]

    def g_view(y, h, half):
        if half is None:
            return gbuf.at[y * 2 + h]
        return gbuf.at[y * 2 + h, pl.ds(half * HALF, HALF)]

    kv[0, here.d] = k_ref[...]
    kv[1, here.d] = v_ref[...]
    gbuf[here.t] = g_ref[...]
    kvg = Gather(lambda z, x, half: kv_view(z, x, here.c, half), here.z, here.x, here.by_dc, kv_s, kv_r)
    sib = Sibling(kv_view, here, sib_s, sib_r)
    gg = Gather(g_view, here.y, here.h, here.by_tp, g_s, g_r)
    zu, zd, _ = around(here.z)
    yu, yd, _ = around(here.y)
    meet([
        here.by_dc(zu, here.x), here.by_dc(zd, here.x), here.by_dc(here.z, 1 - here.x), here.sibling(),
        here.by_tp(yu, here.h), here.by_tp(yd, here.h), here.by_tp(here.y, 1 - here.h),
    ])
    kvg.start()
    sib.start(0)
    gg.start()
    for j in range(8):
        load_w(j).start()
    split_heads(q_s, q_ref)
    write_bias(bias, place_ref, length_ref, here)
    top[...] = jnp.full(top.shape, FILL, F32)
    total[...] = jnp.zeros(total.shape, F32)
    oacc[...] = jnp.zeros(oacc.shape, F32)
    hacc[...] = jnp.zeros(hacc.shape, F32)
    kvg.pair()
    sib.start(1)
    kvg.near()
    sib.start(2, 3)
    kvg.near_pair()
    sib.start(4, 5)
    kvg.far()
    sib.start(6)
    kvg.far_pair()
    sib.start(7)
    sib.got(*range(8))
    gg.near()
    gg.pair()
    copies = pltpu.make_async_copy(kv, kv_out, out_sem)
    copies.start()

    def scores(z, g):
        q = q_s[pl.ds(2 * g, 2)].reshape(2 * ROWS, HEAD_DIM)
        s = dot_nt(q, keys_of(kv, 0, z)) * SCALE2
        s = s.reshape(2, ROWS, ZK) + bias[z][None]
        return s.reshape(2 * ROWS, ZK)

    def maxima(i, carry):
        z, g = lax.div(i, 4), lax.rem(i, 4)
        s = scores(z, g)
        high = top[g]
        for j in range(ZK // 128):
            high = jnp.maximum(high, s[:, j * 128 : (j + 1) * 128])
        top[g] = high
        return carry

    def outputs(i, carry):
        z, g = lax.div(i, 4), lax.rem(i, 4)
        p = jnp.exp2(scores(z, g) - top[g][:, :1])
        part = total[g]
        for j in range(ZK // 128):
            part = part + p[:, j * 128 : (j + 1) * 128]
        total[g] = part
        oacc[g] += dot_nn(p.astype(BF16), keys_of(kv, 1, z))
        return carry

    lax.fori_loop(0, 16, maxima, 0)

    def spread(g, carry):
        top[g] = jnp.broadcast_to(jnp.max(top[g], axis=1, keepdims=True), (2 * ROWS, 128))
        return carry

    lax.fori_loop(0, 4, spread, 0)
    lax.fori_loop(0, 16, outputs, 0)
    for g in range(4):
        whole = jnp.broadcast_to(jnp.sum(total[g], axis=1, keepdims=True), (2 * ROWS, 128))
        lse_ref[g] = top[g] + jnp.log2(whole)
        o = (oacc[g] / whole).astype(BF16)
        for j in range(2):
            head = 2 * g + j
            att_ref[:, head * HEAD_DIM : (head + 1) * HEAD_DIM] = o[j * ROWS : (j + 1) * ROWS]

    gg.near_pair()

    def head_grads(y, h):
        slot = y * 2 + h

        def tile(n, carry):
            cols = pl.ds(pl.multiple_of(n * 256, 256), 256)
            hacc[:, cols] += dot_nt(gbuf[slot], wbuf[slot, cols, :])
            return carry

        lax.fori_loop(0, 4, tile, 0)

    for j in range(8):
        load_w(j).wait()
    far = around(here.y)[2]
    o = 1 - here.h
    for y, h in ((here.y, here.h), (here.y, o), (yd, here.h), (yu, here.h), (yd, o), (yu, o)):
        head_grads(y, h)
    gg.far()
    head_grads(far, here.h)
    gg.far_pair()
    head_grads(far, o)
    hg_ref[...] = hacc[...].astype(BF16)
    copies.wait()
    kvg.drain()
    sib.drain()
    gg.drain()


def backward_kernel(
    q_ref, kv, att_ref, hg_ref, lse_ref, same_ref, cross_ref, w_ref, place_ref, length_ref,
    out_ref, dq_ref, dk_ref, dv_ref, gw_ref,
    attall, gcol, wbuf, q_s, do_s, qt_s, dot_s, delta, bias, dqacc, kt, vt, keep, sib_out, sib_in,
    c_out, c_in, d_out, d_in, d_final, gacc,
    wsem, att_s, att_r, sib_s, sib_r, col_s, col_r, c_s, c_r, x_s, x_r, d_s, d_r,
):
    here = Here()

    def load_w(j):
        return pltpu.make_async_copy(w_ref.at[:, pl.ds(j * COLS, COLS)], wbuf.at[j], wsem.at[j])

    for j in range(8):
        load_w(j).start()

    def att_view(z, x, core, half=None):
        slot = (z * 2 + x) * 2 + core
        if half is None:
            return attall.at[slot]
        return attall.at[slot, pl.ds(half * HALF, HALF)]

    def col_view(y, h, half):
        if half is None:
            return gcol.at[y * 2 + h]
        return gcol.at[y * 2 + h, half]

    attall[here.d] = att_ref[...]
    gcol[here.t, here.c] = same_ref[...]
    gcol[here.t, 1 - here.c] = cross_ref[...]
    ag = Gather(lambda z, x, half: att_view(z, x, here.c, half), here.z, here.x, here.by_dc, att_s, att_r)
    sib = Sibling(att_view, here, sib_s, sib_r)
    cg = Gather(col_view, here.y, here.h, here.by_tp, col_s, col_r)
    zu, zd, zf = around(here.z)
    yu, yd, yf = around(here.y)
    meet([
        here.by_dc(zu, here.x), here.by_dc(zd, here.x), here.by_dc(here.z, 1 - here.x), here.sibling(),
        here.by_tp(yu, here.h), here.by_tp(yd, here.h), here.by_tp(here.y, 1 - here.h),
    ])
    ag.start()
    sib.start(0)

    def out_part(dst, which, h, adds):
        slot = {"far": yf, "up": yu, "dn": yd, "own": here.y}[which] * 2 + h

        def tile(n, carry):
            cols = pl.ds(pl.multiple_of(n * 256, 256), 256)
            acc = dot_nn(att_ref[...], wbuf[slot, :, cols])
            for add in adds:
                acc = acc + add[:, cols].astype(F32)
            dst[:, cols] = acc.astype(BF16)
            return carry

        lax.fori_loop(0, 4, tile, 0)

    c_red = Reduce(out_part, here.y, here.h, here.by_tp, c_out, c_in, c_s, c_r)

    def kv_part(dst, which, x, adds):
        r = {"far": 0, "dn": 1, "up": 2, "own": 3}[which]
        acc = keep[r, x] + sib_in[r, x].astype(F32)
        for add in adds:
            acc = acc + add[...].astype(F32)
        dst[...] = acc.astype(BF16)

    d_red = Reduce(kv_part, here.z, here.x, here.by_dc, d_out, d_in, d_s, d_r)

    def sib_sum(r):
        return pltpu.make_async_remote_copy(
            sib_out.at[r], sib_in.at[r], x_s.at[r], x_r.at[r],
            device_id=here.sibling(), device_id_type=MESH,
        )

    for j in range(8):
        load_w(j).wait()
    c_red.far()
    c_red.near()
    cg.start()

    split_heads(q_s, q_ref)
    split_heads(do_s, hg_ref)
    write_bias(bias, place_ref, length_ref, here)
    dqacc[...] = jnp.zeros(dqacc.shape, F32)
    for g in range(4):
        for j in range(2):
            head = 2 * g + j
            a = att_ref[:, head * HEAD_DIM : (head + 1) * HEAD_DIM].astype(F32)
            d = do_s[head].astype(F32)
            delta[g, pl.ds(j * ROWS, ROWS)] = jnp.broadcast_to(
                jnp.sum(a * d, axis=1, keepdims=True), (ROWS, 128)
            )
        qt_s[g] = q_s[pl.ds(2 * g, 2)].reshape(2 * ROWS, HEAD_DIM).T
        dot_s[g] = do_s[pl.ds(2 * g, 2)].reshape(2 * ROWS, HEAD_DIM).T

    def plane(r, z):
        kt[...] = jnp.zeros(kt.shape, F32)
        vt[...] = jnp.zeros(vt.shape, F32)

        def step(g, carry):
            k, v = keys_of(kv, 0, z), keys_of(kv, 1, z)
            q = q_s[pl.ds(2 * g, 2)].reshape(2 * ROWS, HEAD_DIM)
            do = do_s[pl.ds(2 * g, 2)].reshape(2 * ROWS, HEAD_DIM)
            s = dot_nt(q, k) * SCALE2
            s = (s.reshape(2, ROWS, ZK) + bias[z][None]).reshape(2 * ROWS, ZK)
            p = jnp.exp2(s - lse_ref[g][:, :1])
            ds = (p * (dot_nt(do, v) - delta[g][:, :1])).astype(BF16)
            dqacc[g] += dot_nn(ds, k)
            kt[...] += dot_nn(qt_s[g], ds)
            vt[...] += dot_nn(dot_s[g], p.astype(BF16))
            return carry

        lax.fori_loop(0, 4, step, 0)
        dk = (kt[...] * SCALE).T.reshape(4, ROWS, HEAD_DIM)
        dv = vt[...].T.reshape(4, ROWS, HEAD_DIM)
        for x in range(2):
            mine = here.c == 0
            for which, value in ((0, dk), (1, dv)):
                even, odd = value[2 * x], value[2 * x + 1]
                keep[r, x, which] = jnp.where(mine, even, odd)
                sib_out[r, x, which] = jnp.where(mine, odd, even).astype(BF16)
        sib_sum(r).start()

    plane(0, zf)
    ag.pair()
    sib.start(1)
    ag.near()
    sib.start(2, 3)
    c_red.comb()
    plane(1, zd)
    sib_sum(0).wait_recv()
    d_red.far()
    ag.near_pair()
    sib.start(4, 5)
    cg.pair()
    plane(2, zu)
    sib_sum(1).wait_recv()
    sib_sum(2).wait_recv()
    d_red.near()
    cg.near()
    c_red.pair()
    plane(3, here.z)
    d_red.comb()
    ag.far()
    sib.start(6)
    ag.far_pair()
    sib.start(7)
    cg.near_pair()
    for g in range(4):
        value = (dqacc[g] * SCALE).astype(BF16)
        for j in range(2):
            head = 2 * g + j
            dq_ref[:, head * HEAD_DIM : (head + 1) * HEAD_DIM] = value[j * ROWS : (j + 1) * ROWS]
    sib_sum(3).wait_recv()
    d_red.pair()
    sib.got(*range(8))
    gacc[...] = jnp.zeros(gacc.shape, F32)

    def weight_part(y, h):
        chip = lax.rem(y - here.z + 4, 4) * 2 + h
        right = gcol[y * 2 + h].reshape(2 * ROWS, COLS // 2)

        def tile(n, carry):
            cols = pl.ds(pl.multiple_of(n * 256, 256), 256)
            left = attall[pl.ds(2 * chip, 2), :, cols].reshape(2 * ROWS, 256)
            gacc[cols, :] += dot_tn(left, right)
            return carry

        lax.fori_loop(0, 4, tile, 0)

    o = 1 - here.h
    for y, h in ((here.y, here.h), (here.y, o), (yd, here.h), (yu, here.h), (yd, o), (yu, o)):
        weight_part(y, h)
    d_red.final(d_final)
    dk_ref[...] = d_final[0]
    dv_ref[...] = d_final[1]
    c_red.final(out_ref)
    cg.far()
    weight_part(yf, here.h)
    cg.far_pair()
    weight_part(yf, o)
    gw_ref[...] = gacc[...].astype(BF16)
    ag.drain()
    sib.drain()
    cg.drain()
    c_red.drain()
    d_red.drain()
    for r in range(4):
        sib_sum(r).wait_send()


def vmem():
    return pl.BlockSpec(memory_space=pltpu.VMEM)


def smem():
    return pl.BlockSpec(memory_space=pltpu.SMEM)


def anywhere():
    return pl.BlockSpec(memory_space=pl.ANY)


def dma(n):
    return pltpu.SemaphoreType.DMA((n,))


def forward(q, k, v, w, g, place, length):
    shape = jax.ShapeDtypeStruct
    return pl.pallas_call(
        forward_kernel,
        out_shape=(
            shape((ROWS, COLS), BF16),
            shape((ROWS, COLS), BF16),
            shape((4, 2 * ROWS, 128), F32),
            shape((2, 16, ROWS, HEAD_DIM), BF16),
        ),
        in_specs=[vmem(), vmem(), vmem(), anywhere(), vmem(), smem(), smem()],
        out_specs=(vmem(), vmem(), vmem(), anywhere()),
        scratch_shapes=[
            pltpu.VMEM((2, 16, ROWS, HEAD_DIM), BF16),
            pltpu.VMEM((8, ROWS, COLS), BF16),
            pltpu.VMEM((8, COLS, COLS), BF16),
            pltpu.VMEM((GROUP, ROWS, HEAD_DIM), BF16),
            pltpu.VMEM((4, ROWS, ZK), F32),
            pltpu.VMEM((4, 2 * ROWS, 128), F32),
            pltpu.VMEM((4, 2 * ROWS, 128), F32),
            pltpu.VMEM((4, 2 * ROWS, 128), F32),
            pltpu.VMEM((ROWS, COLS), F32),
            dma(8), dma(9), dma(9), dma(8), dma(8), dma(9), dma(9),
            pltpu.SemaphoreType.DMA,
        ],
        compiler_params=pltpu.CompilerParams(
            collective_id=0, has_side_effects=True, vmem_limit_bytes=58 * 2**20
        ),
        cost_estimate=pl.CostEstimate(flops=9 * 10**9, bytes_accessed=24 * 10**6, transcendentals=6 * 10**6),
    )(q, k, v, w, g, place, length)


def backward(q, kv, att, hg, lse, same, cross, w, place, length):
    shape = jax.ShapeDtypeStruct
    return pl.pallas_call(
        backward_kernel,
        out_shape=(
            shape((ROWS, COLS), BF16),
            shape((ROWS, COLS), BF16),
            shape((ROWS, HEAD_DIM), BF16),
            shape((ROWS, HEAD_DIM), BF16),
            shape((COLS, COLS // 2), BF16),
        ),
        in_specs=[vmem()] * 7 + [anywhere(), smem(), smem()],
        out_specs=(vmem(),) * 5,
        scratch_shapes=[
            pltpu.VMEM((16, ROWS, COLS), BF16),
            pltpu.VMEM((8, 2, ROWS, COLS // 2), BF16),
            pltpu.VMEM((8, COLS, COLS), BF16),
            pltpu.VMEM((GROUP, ROWS, HEAD_DIM), BF16),
            pltpu.VMEM((GROUP, ROWS, HEAD_DIM), BF16),
            pltpu.VMEM((4, HEAD_DIM, 2 * ROWS), BF16),
            pltpu.VMEM((4, HEAD_DIM, 2 * ROWS), BF16),
            pltpu.VMEM((4, 2 * ROWS, 128), F32),
            pltpu.VMEM((4, ROWS, ZK), F32),
            pltpu.VMEM((4, 2 * ROWS, 128), F32),
            pltpu.VMEM((HEAD_DIM, ZK), F32),
            pltpu.VMEM((HEAD_DIM, ZK), F32),
            pltpu.VMEM((4, 2, 2, ROWS, HEAD_DIM), F32),
            pltpu.VMEM((4, 2, 2, ROWS, HEAD_DIM), BF16),
            pltpu.VMEM((4, 2, 2, ROWS, HEAD_DIM), BF16),
            pltpu.VMEM((7, ROWS, COLS), BF16),
            pltpu.VMEM((7, ROWS, COLS), BF16),
            pltpu.VMEM((7, 2, ROWS, HEAD_DIM), BF16),
            pltpu.VMEM((7, 2, ROWS, HEAD_DIM), BF16),
            pltpu.VMEM((2, ROWS, HEAD_DIM), BF16),
            pltpu.VMEM((COLS, COLS // 2), F32),
            dma(8), dma(9), dma(9), dma(8), dma(8), dma(9), dma(9), dma(7), dma(7), dma(4), dma(4),
            dma(7), dma(7),
        ],
        compiler_params=pltpu.CompilerParams(
            collective_id=1, has_side_effects=True, vmem_limit_bytes=62 * 2**20
        ),
        cost_estimate=pl.CostEstimate(flops=16 * 10**9, bytes_accessed=30 * 10**6, transcendentals=6 * 10**6),
    )(q, kv, att, hg, lse, same, cross, w, place, length)


def permutation(flip):
    pairs = []
    for d in range(16):
        z, x, c = d // 4, d // 2 % 2, d % 2
        for t in range(8):
            y, h = t // 2, t % 2
            to = ((y * 2 + h) * 2 + (c ^ flip)) * 8 + (y + z) % 4 * 2 + x
            pairs.append((d * 8 + t, to))
    return pairs


def on_device(q, k, v, w, g, place, length):
    core = lax.rem(lax.axis_index("dc"), 2)
    half = COLS // 2
    same = lax.ppermute(
        lax.dynamic_slice_in_dim(g, core * half, half, axis=1), ("dc", "tp"), permutation(0)
    )
    cross = lax.ppermute(
        lax.dynamic_slice_in_dim(g, (1 - core) * half, half, axis=1), ("dc", "tp"), permutation(1)
    )
    att, hg, lse, kv = forward(q, k, v, w, g, place, length)
    return backward(q, kv, att, hg, lse, same, cross, w, place, length)


def solution(mesh):
    in_specs = (P("dc", "tp"), P("dc", "tp"), P("dc", "tp"), P("tp", None), P("dc", "tp"), P(), P())
    out_specs = (P("dc", "tp"), P("dc", "tp"), P("dc", "tp"), P("dc", "tp"), P("tp", "dc"))
    return jax.shard_map(
        on_device, mesh=mesh, in_specs=in_specs, out_specs=out_specs, check_vma=False
    )
```

```python
import jax
import jax.numpy as jnp
from jax import lax
from jax.experimental import pallas as pl
from jax.experimental.pallas import tpu as pltpu
from jax.sharding import PartitionSpec as P

HEAD_DIM = 128
ROWS = 224
SPAN = 112
GROUP = 8
ZK = 896
COLS = 1024
SCALE = HEAD_DIM**-0.5
SCALE2 = SCALE * 1.4426950408889634
FILL = -1e30
MESH = pl.DeviceIdType.MESH
F32 = jnp.float32
BF16 = jnp.bfloat16


def dot_nn(a, b):
    return lax.dot_general(a, b, (((1,), (0,)), ((), ())), preferred_element_type=F32)


def dot_nt(a, b):
    return lax.dot_general(a, b, (((1,), (1,)), ((), ())), preferred_element_type=F32)


def dot_tn(a, b):
    return lax.dot_general(a, b, (((0,), (0,)), ((), ())), preferred_element_type=F32)


class Here:
    def __init__(self):
        d = lax.axis_index("dc")
        t = lax.axis_index("tp")
        self.d, self.t = d, t
        self.c = lax.rem(d, 2)
        self.x = lax.rem(lax.div(d, 2), 2)
        self.z = lax.div(d, 4)
        self.h = lax.rem(t, 2)
        self.y = lax.div(t, 2)

    def by_dc(self, z, x):
        return ((z * 2 + x) * 2 + self.c, self.t)

    def by_tp(self, y, h):
        return (self.d, y * 2 + h)

    def sibling(self):
        return ((self.z * 2 + self.x) * 2 + (1 - self.c), self.t)


def around(a):
    return lax.rem(a + 1, 4), lax.rem(a + 3, 4), lax.rem(a + 2, 4)


def meet(devices):
    barrier = pltpu.get_barrier_semaphore()
    for device in devices:
        pl.semaphore_signal(barrier, inc=1, device_id=device, device_id_type=MESH)
    pl.semaphore_wait(barrier, len(devices))


class Gather:
    def __init__(self, view, a, b, dev, ssem, rsem, rows, cross=0):
        up, dn, far = around(a)
        o = 1 - b
        self.view, self.ssem, self.rsem = view, ssem, rsem
        self.count = 12 if cross else 9
        half, some = rows // 2, (rows - cross) // 2
        whole, low, high = (0, rows), (0, half), (half, half)
        rest, first, second = (cross, rows - cross), (cross, some), (cross + some, some)
        over = (0, cross)
        self.out = [
            (a, b, whole, dev(a, o)),
            (a, b, whole, dev(up, b)),
            (a, b, whole, dev(dn, b)),
            (a, o, rest, dev(up, b)),
            (a, o, rest, dev(dn, b)),
            (dn, b, low, dev(up, b)),
            (up, b, high, dev(dn, b)),
            (dn, o, first, dev(up, b)),
            (up, o, second, dev(dn, b)),
            (dn, b, over, dev(a, o)),
            (up, b, over, dev(a, o)),
            (far, b, over, dev(a, o)),
        ]
        self.into = [
            (a, o, whole),
            (dn, b, whole),
            (up, b, whole),
            (dn, o, rest),
            (up, o, rest),
            (far, b, low),
            (far, b, high),
            (far, o, first),
            (far, o, second),
            (dn, o, over),
            (up, o, over),
            (far, o, over),
        ]

    def copy(self, i, part):
        ref = self.view(*part)
        return pltpu.make_async_remote_copy(
            ref, ref, self.ssem.at[i], self.rsem.at[i],
            device_id=self.out[i][3], device_id_type=MESH,
        )

    def send(self, *order):
        for i in order:
            if i < self.count:
                a, b, (first, rows), _ = self.out[i]
                self.copy(i, (a, b, first, rows)).start()

    def got(self, *order):
        for i in order:
            if i < self.count:
                a, b, (first, rows) = self.into[i]
                self.copy(i, (a, b, first, rows)).wait_recv()

    def start(self):
        self.send(1, 2, 0)

    def pair(self):
        self.got(0)
        self.send(3, 4)

    def near(self):
        self.got(1)
        self.send(5, 9)
        self.got(2)
        self.send(6, 10)

    def near_pair(self):
        self.got(3)
        self.send(7)
        self.got(4)
        self.send(8)

    def far(self):
        self.got(5)
        self.send(11)
        self.got(6)

    def near_over(self):
        self.got(9, 10)

    def far_pair(self):
        self.got(7, 8, 11)

    def drain(self):
        for i in range(self.count):
            a, b, (first, rows), _ = self.out[i]
            self.copy(i, (a, b, first, rows)).wait_send()


class Sibling:
    def __init__(self, view, here, ssem, rsem):
        up, dn, far = around(here.z)
        x, o = here.x, 1 - here.x
        self.here, self.view, self.ssem, self.rsem = here, view, ssem, rsem
        self.blocks = [
            (here.z, x), (here.z, o), (dn, x), (up, x), (dn, o), (up, o), (far, x), (far, o),
        ]

    def sent(self, i, core):
        z, x = self.blocks[i]
        ref = self.view(z, x, core)
        return pltpu.make_async_remote_copy(
            ref, ref, self.ssem.at[i], self.rsem.at[i],
            device_id=self.here.sibling(), device_id_type=MESH,
        )

    def start(self, *order):
        for i in order:
            self.sent(i, self.here.c).start()

    def got(self, *order):
        for i in order:
            self.sent(i, 1 - self.here.c).wait_recv()

    def drain(self):
        for i in range(8):
            self.sent(i, self.here.c).wait_send()


class Reduce:
    def __init__(self, emit, a, b, dev, sbuf, rbuf, ssem, rsem):
        up, dn, far = around(a)
        self.emit, self.b, self.sbuf, self.rbuf, self.ssem, self.rsem = emit, b, sbuf, rbuf, ssem, rsem
        u, d, p = dev(up, b), dev(dn, b), dev(a, 1 - b)
        self.devices = [u, d, u, d, u, d, p]

    def copy(self, i):
        return pltpu.make_async_remote_copy(
            self.sbuf.at[i], self.rbuf.at[i], self.ssem.at[i], self.rsem.at[i],
            device_id=self.devices[i], device_id_type=MESH,
        )

    def send(self, i, which, b, adds=()):
        self.emit(self.sbuf.at[i], which, b, [self.rbuf.at[j] for j in adds])
        self.copy(i).start()

    def far(self):
        self.send(0, "far", 0)
        self.send(1, "far", 1)

    def near(self):
        self.send(2, "up", 1)
        self.send(3, "dn", 0)

    def comb(self):
        self.copy(0).wait_recv()
        self.send(4, "up", 0, [0])
        self.copy(1).wait_recv()
        self.send(5, "dn", 1, [1])

    def pair(self):
        for i in (2, 3, 4, 5):
            self.copy(i).wait_recv()
        o = 1 - self.b
        self.send(6, "own", o, [4 + o, 3 - o])

    def final(self, out):
        self.copy(6).wait_recv()
        b = self.b
        self.emit(out, "own", b, [self.rbuf.at[j] for j in (4 + b, 3 - b, 6)])

    def drain(self):
        for i in range(7):
            self.copy(i).wait_send()


def write_bias(bias, place_ref, length_ref, here):
    row = lax.broadcasted_iota(jnp.int32, (ROWS, 1), 0)
    first, second = place_ref[2 * here.d], place_ref[2 * here.d + 1]
    pos = row + jnp.where(row < SPAN, first * SPAN, second * SPAN - SPAN)
    low = jnp.zeros((ROWS, 1), jnp.int32)
    bound = length_ref[0]
    for i in range(1, 4):
        low = jnp.where(pos >= bound, bound, low)
        bound = bound + length_ref[i]

    def fill(z, carry):
        lane = lax.broadcasted_iota(jnp.int32, (1, ZK), 1)
        key = jnp.zeros((1, ZK), jnp.int32)
        for i in range(8):
            begin = place_ref[8 * z + i] * SPAN - i * SPAN
            key = jnp.where(lane >= i * SPAN, lane + begin, key)
        bias[z] = jnp.where((key >= low) & (key <= pos), 0.0, FILL)
        return carry

    lax.fori_loop(0, 4, fill, 0)


def split_heads(dst, src):
    for head in range(GROUP):
        dst[head] = src[:, head * HEAD_DIM : (head + 1) * HEAD_DIM]


def keys_of(kv, which, z):
    return kv[which, pl.ds(4 * z, 4)].reshape(ZK, HEAD_DIM)


def shifted(z):
    return jnp.where(z == 0, 1, jnp.where(z == 1, 3, jnp.where(z == 2, 2, 0)))


def layer_kernel(
    q_ref, k_ref, v_ref, w_ref, g_ref, place_ref, length_ref,
    out_ref, dq_ref, dk_ref, dv_ref, gw_ref,
    kv, gbuf, wbuf, attall, gcol, q_s, do_s, qt_s, dot_s, bias, top, total, oacc, hacc,
    kt, vt, keep, sib_out, sib_in, c_out, c_in, d_out, d_in, d_final, gacc,
    wsem, kv_s, kv_r, kvsib_s, kvsib_r, g_s, g_r, per_s, per_r, att_s, att_r, sib_s, sib_r,
    col_s, col_r, c_s, c_r, x_s, x_r, d_s, d_r,
):
    here = Here()
    zu, zd, zf = around(here.z)
    yu, yd, yf = around(here.y)
    h, o = here.h, 1 - here.h
    half = COLS // 2

    def load_w(j):
        return pltpu.make_async_copy(w_ref.at[:, pl.ds(j * COLS, COLS)], wbuf.at[j], wsem.at[j])

    for j in range(8):
        load_w(j).start()

    def kv_view(z, x, first, rows):
        return kv.at[:, (z * 2 + x) * 2 + here.c, pl.ds(first, rows)]

    def att_view(z, x, first, rows):
        return attall.at[(z * 2 + x) * 2 + here.c, pl.ds(first, rows)]

    kvg = Gather(kv_view, here.z, here.x, here.by_dc, kv_s, kv_r, ROWS)
    kvsib = Sibling(lambda z, x, core: kv.at[:, (z * 2 + x) * 2 + core], here, kvsib_s, kvsib_r)
    gg = Gather(
        lambda y, h, first, rows: gbuf.at[y * 2 + h, pl.ds(first, rows)],
        here.y, h, here.by_tp, g_s, g_r, ROWS, 64,
    )
    ag = Gather(att_view, here.z, here.x, here.by_dc, att_s, att_r, ROWS)
    sib = Sibling(lambda z, x, core: attall.at[(z * 2 + x) * 2 + core], here, sib_s, sib_r)
    cg = Gather(
        lambda y, h, first, rows: gcol.at[y * 2 + h, pl.ds(first, rows)],
        here.y, h, here.by_tp, col_s, col_r, 2 * ROWS, 128,
    )

    to_y = lax.rem(shifted(here.y) - here.z + 4, 4)
    from_z = lax.rem(shifted(here.z) - here.y + 4, 4)

    def to_chip(core):
        return ((here.y * 2 + h) * 2 + core, to_y * 2 + here.x)

    def from_chip(core):
        return ((from_z * 2 + h) * 2 + core, here.z * 2 + here.x)

    def handed(i):
        core = here.c if i == 0 else 1 - here.c
        cols = pl.ds(pl.multiple_of(core * half, half), half)
        rows = pl.ds(pl.multiple_of(here.c * ROWS, ROWS), ROWS)
        return pltpu.make_async_remote_copy(
            g_ref.at[:, cols], gcol.at[to_y * 2 + here.x, rows], per_s.at[i], per_r.at[i],
            device_id=to_chip(core), device_id_type=MESH,
        )

    def taken(i):
        core = here.c if i == 0 else 1 - here.c
        rows = pl.ds(pl.multiple_of(core * ROWS, ROWS), ROWS)
        ref = gcol.at[here.t, rows]
        pltpu.make_async_remote_copy(
            ref, ref, per_s.at[i], per_r.at[i], device_id=from_chip(core), device_id_type=MESH
        ).wait_recv()

    kv[0, here.d] = k_ref[...]
    kv[1, here.d] = v_ref[...]
    gbuf[here.t] = g_ref[...]
    meet(
        [
            here.by_dc(zu, here.x), here.by_dc(zd, here.x), here.by_dc(here.z, 1 - here.x), here.sibling(),
            here.by_tp(yu, h), here.by_tp(yd, h), here.by_tp(here.y, o),
            from_chip(here.c), from_chip(1 - here.c),
        ]
    )
    kvg.start()
    kvsib.start(0)
    gg.start()
    handed(0).start()
    handed(1).start()
    split_heads(q_s, q_ref)
    write_bias(bias, place_ref, length_ref, here)
    top[...] = jnp.full(top.shape, FILL, F32)
    total[...] = jnp.zeros(total.shape, F32)
    oacc[...] = jnp.zeros(oacc.shape, F32)
    hacc[...] = jnp.zeros(hacc.shape, F32)

    def scores(z, g):
        q = q_s[pl.ds(2 * g, 2)].reshape(2 * ROWS, HEAD_DIM)
        s = dot_nt(q, keys_of(kv, 0, z)) * SCALE2
        s = s.reshape(2, ROWS, ZK) + bias[z][None]
        return s.reshape(2 * ROWS, ZK)

    def attend(z):
        def step(g, carry):
            s = scores(z, g)
            high = s[:, :128]
            for j in range(1, ZK // 128):
                high = jnp.maximum(high, s[:, j * 128 : (j + 1) * 128])
            old = top[g]
            new = jnp.maximum(old, jnp.max(high, axis=1, keepdims=True))
            p = jnp.exp2(s - new[:, :1])
            alpha = jnp.exp2(old - new)
            part = total[g] * alpha
            for j in range(ZK // 128):
                part = part + p[:, j * 128 : (j + 1) * 128]
            total[g] = part
            top[g] = new
            oacc[g] = oacc[g] * alpha + dot_nn(p.astype(BF16), keys_of(kv, 1, z))
            return carry

        lax.fori_loop(0, 4, step, 0)

    def head_grads(y, h):
        slot = y * 2 + h

        def tile(n, carry):
            rows = pl.ds(pl.multiple_of(n * 256, 256), 256)
            hacc[rows, :] += dot_nt(wbuf[slot, rows, :], gbuf[slot])
            return carry

        lax.fori_loop(0, 4, tile, 0)

    def out_part(dst, which, h, adds):
        slot = {"far": yf, "up": yu, "dn": yd, "own": here.y}[which] * 2 + h

        def tile(n, carry):
            cols = pl.ds(pl.multiple_of(n * 256, 256), 256)
            acc = dot_nn(attall[here.d], wbuf[slot, :, cols])
            for add in adds:
                acc = acc + add[:, cols].astype(F32)
            dst[:, cols] = acc.astype(BF16)
            return carry

        lax.fori_loop(0, 4, tile, 0)

    def kv_part(dst, which, x, adds):
        r = {"far": 0, "dn": 1, "up": 2, "own": 3}[which]
        acc = keep[r, x] + sib_in[r, x].astype(F32)
        for add in adds:
            acc = acc + add[...].astype(F32)
        dst[...] = acc.astype(BF16)

    c_red = Reduce(out_part, here.y, h, here.by_tp, c_out, c_in, c_s, c_r)
    d_red = Reduce(kv_part, here.z, here.x, here.by_dc, d_out, d_in, d_s, d_r)

    def sib_sum(r):
        return pltpu.make_async_remote_copy(
            sib_out.at[r], sib_in.at[r], x_s.at[r], x_r.at[r],
            device_id=here.sibling(), device_id_type=MESH,
        )

    def plane(r, z):
        kt[...] = jnp.zeros(kt.shape, F32)
        vt[...] = jnp.zeros(vt.shape, F32)

        def step(g, carry):
            k, v = keys_of(kv, 0, z), keys_of(kv, 1, z)
            do = do_s[pl.ds(2 * g, 2)].reshape(2 * ROWS, HEAD_DIM)
            p = jnp.exp2(scores(z, g) - top[g][:, :1])
            ds = (p * (dot_nt(do, v) - total[g][:, :1])).astype(BF16)
            oacc[g] += dot_nn(ds, k)
            kt[...] += dot_nn(qt_s[g], ds)
            vt[...] += dot_nn(dot_s[g], p.astype(BF16))
            return carry

        lax.fori_loop(0, 4, step, 0)
        dk = (kt[...] * SCALE).T.reshape(4, ROWS, HEAD_DIM)
        dv = vt[...].T.reshape(4, ROWS, HEAD_DIM)
        for x in range(2):
            mine = here.c == 0
            for which, value in ((0, dk), (1, dv)):
                even, odd = value[2 * x], value[2 * x + 1]
                keep[r, x, which] = jnp.where(mine, even, odd)
                sib_out[r, x, which] = jnp.where(mine, odd, even).astype(BF16)
        sib_sum(r).start()

    def weight_part(y, h):
        chip = lax.rem(shifted(here.z) - y + 4, 4) * 2 + h
        right = gcol[y * 2 + h]

        def tile(n, carry):
            cols = pl.ds(pl.multiple_of(n * 256, 256), 256)
            left = attall[pl.ds(2 * chip, 2), :, cols].reshape(2 * ROWS, 256)
            gacc[cols, :] += dot_tn(left, right)
            return carry

        lax.fori_loop(0, 4, tile, 0)

    def finish_attention():
        for g in range(4):
            whole = jnp.broadcast_to(jnp.sum(total[g], axis=1, keepdims=True), (2 * ROWS, 128))
            top[g] = top[g] + jnp.log2(whole)
            value = (oacc[g] / whole).astype(BF16)
            for j in range(2):
                head = 2 * g + j
                attall[here.d, :, head * HEAD_DIM : (head + 1) * HEAD_DIM] = value[j * ROWS : (j + 1) * ROWS]

    def prepare_backward():
        for g in range(4):
            for j in range(2):
                head = 2 * g + j
                grads = hacc[pl.ds(head * HEAD_DIM, HEAD_DIM), :]
                dot_s[g, :, j * ROWS : (j + 1) * ROWS] = grads.astype(BF16)
                do = grads.T.astype(BF16)
                do_s[head] = do
                a = attall[here.d, :, head * HEAD_DIM : (head + 1) * HEAD_DIM].astype(F32)
                total[g, pl.ds(j * ROWS, ROWS)] = jnp.broadcast_to(
                    jnp.sum(a * do.astype(F32), axis=1, keepdims=True), (ROWS, 128)
                )
            qt_s[g] = q_s[pl.ds(2 * g, 2)].reshape(2 * ROWS, HEAD_DIM).T
        oacc[...] = jnp.zeros(oacc.shape, F32)

    def write_grad_queries():
        for g in range(4):
            value = (oacc[g] * SCALE).astype(BF16)
            for j in range(2):
                head = 2 * g + j
                dq_ref[:, head * HEAD_DIM : (head + 1) * HEAD_DIM] = value[j * ROWS : (j + 1) * ROWS]

    def write_grad_keys_values():
        d_red.final(d_final)
        dk_ref[...] = d_final[0]
        dv_ref[...] = d_final[1]

    def wait_w():
        for j in range(8):
            load_w(j).wait()

    def take():
        taken(0)
        taken(1)

    def clear():
        gacc[...] = jnp.zeros(gacc.shape, F32)

    def summed(*order):
        for r in order:
            sib_sum(r).wait_recv()

    def write_grad_weight():
        gw_ref[...] = gacc[...].astype(BF16)

    def drain():
        for group in (kvg, kvsib, gg, ag, sib, cg, c_red, d_red):
            group.drain()
        for i in range(2):
            handed(i).wait_send()
        for r in range(4):
            sib_sum(r).wait_send()

    steps = [
        (kvg.pair,),
        (kvsib.start, 1),
        (kvg.near,),
        (kvsib.start, 2, 3),
        (kvsib.got, 0, 1),
        (attend, here.z),
        (kvg.near_pair,),
        (kvsib.start, 4, 5),
        (kvg.far,),
        (kvsib.start, 6),
        (kvsib.got, 2, 4),
        (attend, zd),
        (kvg.far_pair,),
        (kvsib.start, 7),
        (kvsib.got, 3, 5),
        (attend, zu),
        (gg.near,),
        (gg.pair,),
        (kvsib.got, 6, 7),
        (attend, zf),
        (finish_attention,),
        (ag.start,),
        (sib.start, 0),
        (wait_w,),
        (c_red.far,),
        (gg.near_pair,),
        (c_red.near,),
        (gg.far,),
        (take,),
        (cg.start,),
        (head_grads, here.y, h),
        (head_grads, here.y, o),
        (head_grads, yd, h),
        (head_grads, yu, h),
        (ag.pair,),
        (sib.start, 1),
        (ag.near,),
        (sib.start, 2, 3),
        (gg.near_over,),
        (head_grads, yd, o),
        (head_grads, yu, o),
        (head_grads, yf, h),
        (gg.far_pair,),
        (head_grads, yf, o),
        (prepare_backward,),
        (c_red.comb,),
        (plane, 0, zf),
        (ag.near_pair,),
        (sib.start, 4, 5),
        (cg.near,),
        (cg.pair,),
        (plane, 1, zd),
        (summed, 0),
        (d_red.far,),
        (ag.far,),
        (sib.start, 6),
        (plane, 2, zu),
        (ag.far_pair,),
        (sib.start, 7),
        (summed, 1, 2),
        (d_red.near,),
        (cg.near_pair,),
        (plane, 3, here.z),
        (d_red.comb,),
        (c_red.pair,),
        (write_grad_queries,),
        (summed, 3),
        (d_red.pair,),
        (sib.got, *range(8)),
        (clear,),
        (cg.far,),
        (weight_part, here.y, h),
        (weight_part, here.y, o),
        (weight_part, yd, h),
        (weight_part, yu, h),
        (write_grad_keys_values,),
        (cg.near_over,),
        (weight_part, yd, o),
        (weight_part, yu, o),
        (weight_part, yf, h),
        (c_red.final, out_ref),
        (cg.far_pair,),
        (weight_part, yf, o),
        (write_grad_weight,),
        (drain,),
    ]
    for step, *given in steps:
        step(*given)


def vmem():
    return pl.BlockSpec(memory_space=pltpu.VMEM)


def smem():
    return pl.BlockSpec(memory_space=pltpu.SMEM)


def anywhere():
    return pl.BlockSpec(memory_space=pl.ANY)


def dma(n):
    return pltpu.SemaphoreType.DMA((n,))


def result_shapes():
    shape = jax.ShapeDtypeStruct
    return (
        shape((ROWS, COLS), BF16),
        shape((ROWS, COLS), BF16),
        shape((ROWS, HEAD_DIM), BF16),
        shape((ROWS, HEAD_DIM), BF16),
        shape((COLS, COLS // 2), BF16),
    )


def layer(q, k, v, w, g, place, length):
    return pl.pallas_call(
        layer_kernel,
        out_shape=result_shapes(),
        in_specs=[vmem(), vmem(), vmem(), anywhere(), vmem(), smem(), smem()],
        out_specs=(vmem(),) * 5,
        scratch_shapes=[
            pltpu.VMEM((2, 16, ROWS, HEAD_DIM), BF16),
            pltpu.VMEM((8, ROWS, COLS), BF16),
            pltpu.VMEM((8, COLS, COLS), BF16),
            pltpu.VMEM((16, ROWS, COLS), BF16),
            pltpu.VMEM((8, 2 * ROWS, COLS // 2), BF16),
            pltpu.VMEM((GROUP, ROWS, HEAD_DIM), BF16),
            pltpu.VMEM((GROUP, ROWS, HEAD_DIM), BF16),
            pltpu.VMEM((4, HEAD_DIM, 2 * ROWS), BF16),
            pltpu.VMEM((4, HEAD_DIM, 2 * ROWS), BF16),
            pltpu.VMEM((4, ROWS, ZK), F32),
            pltpu.VMEM((4, 2 * ROWS, 128), F32),
            pltpu.VMEM((4, 2 * ROWS, 128), F32),
            pltpu.VMEM((4, 2 * ROWS, 128), F32),
            pltpu.VMEM((COLS, ROWS), F32),
            pltpu.VMEM((HEAD_DIM, ZK), F32),
            pltpu.VMEM((HEAD_DIM, ZK), F32),
            pltpu.VMEM((4, 2, 2, ROWS, HEAD_DIM), F32),
            pltpu.VMEM((4, 2, 2, ROWS, HEAD_DIM), BF16),
            pltpu.VMEM((4, 2, 2, ROWS, HEAD_DIM), BF16),
            pltpu.VMEM((7, ROWS, COLS), BF16),
            pltpu.VMEM((7, ROWS, COLS), BF16),
            pltpu.VMEM((7, 2, ROWS, HEAD_DIM), BF16),
            pltpu.VMEM((7, 2, ROWS, HEAD_DIM), BF16),
            pltpu.VMEM((2, ROWS, HEAD_DIM), BF16),
            pltpu.VMEM((COLS, COLS // 2), F32),
            dma(8), dma(9), dma(9), dma(8), dma(8), dma(12), dma(12), dma(2), dma(2),
            dma(9), dma(9), dma(8), dma(8), dma(12), dma(12), dma(7), dma(7), dma(4), dma(4),
            dma(7), dma(7),
        ],
        compiler_params=pltpu.CompilerParams(
            collective_id=0, has_side_effects=True, vmem_limit_bytes=63 * 2**20
        ),
        cost_estimate=pl.CostEstimate(flops=24 * 10**9, bytes_accessed=24 * 10**6, transcendentals=12 * 10**6),
    )(q, k, v, w, g, place, length)


def hand_over_kernel(*refs):
    for source, result in zip(refs[:5], refs[5:]):
        result[...] = source[...]


def hand_over(*arrays):
    return pl.pallas_call(
        hand_over_kernel,
        out_shape=result_shapes(),
        in_specs=[vmem()] * 5,
        out_specs=(vmem(),) * 5,
    )(*arrays)


def on_device(q, k, v, w, g, place, length):
    return hand_over(*layer(q, k, v, w, g, place, length))


def solution(mesh):
    in_specs = (P("dc", "tp"), P("dc", "tp"), P("dc", "tp"), P("tp", None), P("dc", "tp"), P(), P())
    out_specs = (P("dc", "tp"), P("dc", "tp"), P("dc", "tp"), P("dc", "tp"), P("tp", "dc"))
    return jax.shard_map(
        on_device, mesh=mesh, in_specs=in_specs, out_specs=out_specs, check_vma=False
    )
```

```python
import jax
import jax.numpy as jnp
from jax import lax
from jax.experimental import pallas as pl
from jax.experimental.pallas import tpu as pltpu
from jax.sharding import PartitionSpec as P

HEAD_DIM = 128
ROWS = 224
SPAN = 112
GROUP = 8
ZK = 896
COLS = 1024
SCALE = HEAD_DIM**-0.5
SCALE2 = SCALE * 1.4426950408889634
FILL = -1e30
MESH = pl.DeviceIdType.MESH
F32 = jnp.float32
BF16 = jnp.bfloat16


def dot_nn(a, b):
    return lax.dot_general(a, b, (((1,), (0,)), ((), ())), preferred_element_type=F32)


def dot_nt(a, b):
    return lax.dot_general(a, b, (((1,), (1,)), ((), ())), preferred_element_type=F32)


def dot_tn(a, b):
    return lax.dot_general(a, b, (((0,), (0,)), ((), ())), preferred_element_type=F32)


class Here:
    def __init__(self):
        d = lax.axis_index("dc")
        t = lax.axis_index("tp")
        self.d, self.t = d, t
        self.c = lax.rem(d, 2)
        self.x = lax.rem(lax.div(d, 2), 2)
        self.z = lax.div(d, 4)
        self.h = lax.rem(t, 2)
        self.y = lax.div(t, 2)

    def by_dc(self, z, x):
        return ((z * 2 + x) * 2 + self.c, self.t)

    def by_tp(self, y, h):
        return (self.d, y * 2 + h)

    def sibling(self):
        return ((self.z * 2 + self.x) * 2 + (1 - self.c), self.t)


def around(a):
    return lax.rem(a + 1, 4), lax.rem(a + 3, 4), lax.rem(a + 2, 4)


def meet(devices):
    barrier = pltpu.get_barrier_semaphore()
    for device in devices:
        pl.semaphore_signal(barrier, inc=1, device_id=device, device_id_type=MESH)
    pl.semaphore_wait(barrier, len(devices))


class Gather:
    def __init__(self, view, a, b, dev, ssem, rsem, rows, cross=0):
        up, dn, far = around(a)
        o = 1 - b
        self.view, self.ssem, self.rsem = view, ssem, rsem
        self.count = 12 if cross else 9
        half, some = rows // 2, (rows - cross) // 2
        whole, low, high = (0, rows), (0, half), (half, half)
        rest, first, second = (cross, rows - cross), (cross, some), (cross + some, some)
        over = (0, cross)
        self.out = [
            (a, b, whole, dev(a, o)),
            (a, b, whole, dev(up, b)),
            (a, b, whole, dev(dn, b)),
            (a, o, rest, dev(up, b)),
            (a, o, rest, dev(dn, b)),
            (dn, b, low, dev(up, b)),
            (up, b, high, dev(dn, b)),
            (dn, o, first, dev(up, b)),
            (up, o, second, dev(dn, b)),
            (dn, b, over, dev(a, o)),
            (up, b, over, dev(a, o)),
            (far, b, over, dev(a, o)),
        ]
        self.into = [
            (a, o, whole),
            (dn, b, whole),
            (up, b, whole),
            (dn, o, rest),
            (up, o, rest),
            (far, b, low),
            (far, b, high),
            (far, o, first),
            (far, o, second),
            (dn, o, over),
            (up, o, over),
            (far, o, over),
        ]

    def copy(self, i, part):
        ref = self.view(*part)
        return pltpu.make_async_remote_copy(
            ref, ref, self.ssem.at[i], self.rsem.at[i],
            device_id=self.out[i][3], device_id_type=MESH,
        )

    def send(self, *order):
        for i in order:
            if i < self.count:
                a, b, (first, rows), _ = self.out[i]
                self.copy(i, (a, b, first, rows)).start()

    def got(self, *order):
        for i in order:
            if i < self.count:
                a, b, (first, rows) = self.into[i]
                self.copy(i, (a, b, first, rows)).wait_recv()

    def start_pair(self):
        self.send(0)

    def start_near(self):
        self.send(1, 2)

    def pair(self):
        self.got(0)
        self.send(3, 4)

    def near(self):
        self.got(1)
        self.send(5, 9)
        self.got(2)
        self.send(6, 10)

    def near_pair(self):
        self.got(3)
        self.send(7)
        self.got(4)
        self.send(8)

    def far(self):
        self.got(5)
        self.send(11)
        self.got(6)

    def near_over(self):
        self.got(9, 10)

    def far_pair(self):
        self.got(7, 8, 11)

    def drain(self):
        for i in range(self.count):
            a, b, (first, rows), _ = self.out[i]
            self.copy(i, (a, b, first, rows)).wait_send()


class Sibling:
    def __init__(self, view, here, ssem, rsem):
        up, dn, far = around(here.z)
        x, o = here.x, 1 - here.x
        self.here, self.view, self.ssem, self.rsem = here, view, ssem, rsem
        self.blocks = [
            (here.z, x), (here.z, o), (dn, x), (up, x), (dn, o), (up, o), (far, x), (far, o),
        ]

    def sent(self, i, core):
        z, x = self.blocks[i]
        ref = self.view(z, x, core)
        return pltpu.make_async_remote_copy(
            ref, ref, self.ssem.at[i], self.rsem.at[i],
            device_id=self.here.sibling(), device_id_type=MESH,
        )

    def start(self, *order):
        for i in order:
            self.sent(i, self.here.c).start()

    def got(self, *order):
        for i in order:
            self.sent(i, 1 - self.here.c).wait_recv()

    def drain(self):
        for i in range(8):
            self.sent(i, self.here.c).wait_send()


class Reduce:
    def __init__(self, emit, a, b, dev, sbuf, rbuf, ssem, rsem):
        up, dn, far = around(a)
        self.emit, self.b, self.sbuf, self.rbuf, self.ssem, self.rsem = emit, b, sbuf, rbuf, ssem, rsem
        u, d, p = dev(up, b), dev(dn, b), dev(a, 1 - b)
        self.devices = [u, d, u, d, u, d, p]

    def copy(self, i):
        return pltpu.make_async_remote_copy(
            self.sbuf.at[i], self.rbuf.at[i], self.ssem.at[i], self.rsem.at[i],
            device_id=self.devices[i], device_id_type=MESH,
        )

    def send(self, i, which, b, adds=()):
        self.emit(self.sbuf.at[i], which, b, [self.rbuf.at[j] for j in adds])
        self.copy(i).start()

    def far_up(self):
        self.send(0, "far", 0)

    def far_dn(self):
        self.send(1, "far", 1)

    def far(self):
        self.far_up()
        self.far_dn()

    def near_up(self):
        self.send(2, "up", 1)

    def near_dn(self):
        self.send(3, "dn", 0)

    def near(self):
        self.near_up()
        self.near_dn()

    def comb_up(self):
        self.copy(0).wait_recv()
        self.send(4, "up", 0, [0])

    def comb_dn(self):
        self.copy(1).wait_recv()
        self.send(5, "dn", 1, [1])

    def comb(self):
        self.comb_up()
        self.comb_dn()

    def pair(self):
        for i in (2, 3, 4, 5):
            self.copy(i).wait_recv()
        o = 1 - self.b
        self.send(6, "own", o, [4 + o, 3 - o])

    def final(self, out):
        self.copy(6).wait_recv()
        b = self.b
        self.emit(out, "own", b, [self.rbuf.at[j] for j in (4 + b, 3 - b, 6)])

    def drain(self):
        for i in range(7):
            self.copy(i).wait_send()


def write_bias(bias, place_ref, length_ref, here):
    row = lax.broadcasted_iota(jnp.int32, (ROWS, 1), 0)
    first, second = place_ref[2 * here.d], place_ref[2 * here.d + 1]
    pos = row + jnp.where(row < SPAN, first * SPAN, second * SPAN - SPAN)
    low = jnp.zeros((ROWS, 1), jnp.int32)
    bound = length_ref[0]
    for i in range(1, 4):
        low = jnp.where(pos >= bound, bound, low)
        bound = bound + length_ref[i]

    def fill(z, carry):
        lane = lax.broadcasted_iota(jnp.int32, (1, ZK), 1)
        key = jnp.zeros((1, ZK), jnp.int32)
        for i in range(8):
            begin = place_ref[8 * z + i] * SPAN - i * SPAN
            key = jnp.where(lane >= i * SPAN, lane + begin, key)
        bias[z] = jnp.where((key >= low) & (key <= pos), 0.0, FILL)
        return carry

    lax.fori_loop(0, 4, fill, 0)


def split_heads(dst, src):
    for head in range(GROUP):
        dst[head] = src[:, head * HEAD_DIM : (head + 1) * HEAD_DIM]


def keys_of(kv, which, z):
    return kv[which, pl.ds(4 * z, 4)].reshape(ZK, HEAD_DIM)


def shifted(z):
    return jnp.where(z == 0, 1, jnp.where(z == 1, 3, jnp.where(z == 2, 2, 0)))


def layer_kernel(
    q_ref, k_ref, v_ref, w_ref, g_ref, place_ref, length_ref,
    out_ref, dq_ref, dk_ref, dv_ref, gw_ref,
    kv, gbuf, wbuf, attall, gcol, q_s, do_s, qt_s, dot_s, bias, top, total, oacc, hacc,
    kt, vt, keep, sib_out, sib_in, c_out, c_in, d_out, d_in, d_final, gacc,
    wsem, kv_s, kv_r, kvsib_s, kvsib_r, g_s, g_r, per_s, per_r, att_s, att_r, sib_s, sib_r,
    col_s, col_r, c_s, c_r, x_s, x_r, d_s, d_r,
):
    here = Here()
    zu, zd, zf = around(here.z)
    yu, yd, yf = around(here.y)
    h, o = here.h, 1 - here.h
    half = COLS // 2

    def load_w(j):
        return pltpu.make_async_copy(w_ref.at[:, pl.ds(j * COLS, COLS)], wbuf.at[j], wsem.at[j])

    for j in range(8):
        load_w(j).start()

    def kv_view(z, x, first, rows):
        return kv.at[:, (z * 2 + x) * 2 + here.c, pl.ds(first, rows)]

    def att_view(z, x, first, rows):
        return attall.at[(z * 2 + x) * 2 + here.c, pl.ds(first, rows)]

    kvg = Gather(kv_view, here.z, here.x, here.by_dc, kv_s, kv_r, ROWS)
    kvsib = Sibling(lambda z, x, core: kv.at[:, (z * 2 + x) * 2 + core], here, kvsib_s, kvsib_r)
    gg = Gather(
        lambda y, h, first, rows: gbuf.at[y * 2 + h, pl.ds(first, rows)],
        here.y, h, here.by_tp, g_s, g_r, ROWS, 0,
    )
    ag = Gather(att_view, here.z, here.x, here.by_dc, att_s, att_r, ROWS)
    sib = Sibling(lambda z, x, core: attall.at[(z * 2 + x) * 2 + core], here, sib_s, sib_r)
    cg = Gather(
        lambda y, h, first, rows: gcol.at[y * 2 + h, pl.ds(first, rows)],
        here.y, h, here.by_tp, col_s, col_r, 2 * ROWS, 0,
    )

    to_y = lax.rem(shifted(here.y) - here.z + 4, 4)
    from_z = lax.rem(shifted(here.z) - here.y + 4, 4)

    def to_chip(core):
        return ((here.y * 2 + h) * 2 + core, to_y * 2 + here.x)

    def from_chip(core):
        return ((from_z * 2 + h) * 2 + core, here.z * 2 + here.x)

    def handed(i):
        core = here.c if i == 0 else 1 - here.c
        cols = pl.ds(pl.multiple_of(core * half, half), half)
        rows = pl.ds(pl.multiple_of(here.c * ROWS, ROWS), ROWS)
        return pltpu.make_async_remote_copy(
            g_ref.at[:, cols], gcol.at[to_y * 2 + here.x, rows], per_s.at[i], per_r.at[i],
            device_id=to_chip(core), device_id_type=MESH,
        )

    def taken(i):
        core = here.c if i == 0 else 1 - here.c
        rows = pl.ds(pl.multiple_of(core * ROWS, ROWS), ROWS)
        ref = gcol.at[here.t, rows]
        pltpu.make_async_remote_copy(
            ref, ref, per_s.at[i], per_r.at[i], device_id=from_chip(core), device_id_type=MESH
        ).wait_recv()

    kv[0, here.d] = k_ref[...]
    kv[1, here.d] = v_ref[...]
    gbuf[here.t] = g_ref[...]
    meet(
        [
            here.by_dc(zu, here.x), here.by_dc(zd, here.x), here.by_dc(here.z, 1 - here.x), here.sibling(),
            here.by_tp(yu, h), here.by_tp(yd, h), here.by_tp(here.y, o),
            from_chip(here.c), from_chip(1 - here.c),
        ]
    )
    kvg.start_pair()
    kvg.start_near()
    kvsib.start(0)
    gg.start_near()
    split_heads(q_s, q_ref)
    write_bias(bias, place_ref, length_ref, here)
    top[...] = jnp.full(top.shape, FILL, F32)
    total[...] = jnp.zeros(total.shape, F32)
    oacc[...] = jnp.zeros(oacc.shape, F32)
    hacc[...] = jnp.zeros(hacc.shape, F32)

    def scores(z, g):
        q = q_s[pl.ds(2 * g, 2)].reshape(2 * ROWS, HEAD_DIM)
        s = dot_nt(q, keys_of(kv, 0, z)) * SCALE2
        s = s.reshape(2, ROWS, ZK) + bias[z][None]
        return s.reshape(2 * ROWS, ZK)

    def maxima(z):
        def step(g, carry):
            s = scores(z, g)
            high = top[g]
            for j in range(ZK // 128):
                high = jnp.maximum(high, s[:, j * 128 : (j + 1) * 128])
            top[g] = high
            return carry

        lax.fori_loop(0, 4, step, 0)

    def spread():
        def step(g, carry):
            top[g] = jnp.broadcast_to(jnp.max(top[g], axis=1, keepdims=True), (2 * ROWS, 128))
            return carry

        lax.fori_loop(0, 4, step, 0)

    def attend(z):
        def step(g, carry):
            p = jnp.exp2(scores(z, g) - top[g][:, :1])
            part = total[g]
            for j in range(ZK // 128):
                part = part + p[:, j * 128 : (j + 1) * 128]
            total[g] = part
            oacc[g] += dot_nn(p.astype(BF16), keys_of(kv, 1, z))
            return carry

        lax.fori_loop(0, 4, step, 0)

    def head_grads(y, h):
        slot = y * 2 + h

        def tile(n, carry):
            rows = pl.ds(pl.multiple_of(n * 256, 256), 256)
            hacc[rows, :] += dot_nt(wbuf[slot, rows, :], gbuf[slot])
            return carry

        lax.fori_loop(0, 4, tile, 0)

    def out_part(dst, which, h, adds):
        slot = {"far": yf, "up": yu, "dn": yd, "own": here.y}[which] * 2 + h

        def tile(n, carry):
            cols = pl.ds(pl.multiple_of(n * 256, 256), 256)
            acc = dot_nn(attall[here.d], wbuf[slot, :, cols])
            for add in adds:
                acc = acc + add[:, cols].astype(F32)
            dst[:, cols] = acc.astype(BF16)
            return carry

        lax.fori_loop(0, 4, tile, 0)

    def kv_part(dst, which, x, adds):
        r = {"far": 0, "dn": 1, "up": 2, "own": 3}[which]
        acc = keep[r, x] + sib_in[r, x].astype(F32)
        for add in adds:
            acc = acc + add[...].astype(F32)
        dst[...] = acc.astype(BF16)

    c_red = Reduce(out_part, here.y, h, here.by_tp, c_out, c_in, c_s, c_r)
    d_red = Reduce(kv_part, here.z, here.x, here.by_dc, d_out, d_in, d_s, d_r)

    def sib_sum(r):
        return pltpu.make_async_remote_copy(
            sib_out.at[r], sib_in.at[r], x_s.at[r], x_r.at[r],
            device_id=here.sibling(), device_id_type=MESH,
        )

    def plane(z, first):
        def step(g, carry):
            k, v = keys_of(kv, 0, z), keys_of(kv, 1, z)
            do = do_s[pl.ds(2 * g, 2)].reshape(2 * ROWS, HEAD_DIM)
            p = jnp.exp2(scores(z, g) - top[g][:, :1])
            ds = (p * (dot_nt(do, v) - total[g][:, :1])).astype(BF16)
            oacc[g] += dot_nn(ds, k)
            kt[...] += dot_nn(qt_s[g], ds)
            vt[...] += dot_nn(dot_s[g], p.astype(BF16))
            return carry

        lax.fori_loop(first, first + 2, step, 0)

    def plane_a(r, z):
        kt[...] = jnp.zeros(kt.shape, F32)
        vt[...] = jnp.zeros(vt.shape, F32)
        plane(z, 0)

    def plane_b(r, z):
        plane(z, 2)
        dk = (kt[...] * SCALE).T.reshape(4, ROWS, HEAD_DIM)
        dv = vt[...].T.reshape(4, ROWS, HEAD_DIM)
        for x in range(2):
            mine = here.c == 0
            for which, value in ((0, dk), (1, dv)):
                even, odd = value[2 * x], value[2 * x + 1]
                keep[r, x, which] = jnp.where(mine, even, odd)
                sib_out[r, x, which] = jnp.where(mine, odd, even).astype(BF16)
        sib_sum(r).start()

    def weight_part(y, h):
        chip = lax.rem(shifted(here.z) - y + 4, 4) * 2 + h
        right = gcol[y * 2 + h]

        def tile(n, carry):
            cols = pl.ds(pl.multiple_of(n * 256, 256), 256)
            left = attall[pl.ds(2 * chip, 2), :, cols].reshape(2 * ROWS, 256)
            gacc[cols, :] += dot_tn(left, right)
            return carry

        lax.fori_loop(0, 4, tile, 0)

    def finish_attention():
        for g in range(4):
            whole = jnp.broadcast_to(jnp.sum(total[g], axis=1, keepdims=True), (2 * ROWS, 128))
            top[g] = top[g] + jnp.log2(whole)
            value = (oacc[g] / whole).astype(BF16)
            for j in range(2):
                head = 2 * g + j
                attall[here.d, :, head * HEAD_DIM : (head + 1) * HEAD_DIM] = value[j * ROWS : (j + 1) * ROWS]

    def prepare_backward():
        for g in range(4):
            for j in range(2):
                head = 2 * g + j
                grads = hacc[pl.ds(head * HEAD_DIM, HEAD_DIM), :]
                dot_s[g, :, j * ROWS : (j + 1) * ROWS] = grads.astype(BF16)
                do = grads.T.astype(BF16)
                do_s[head] = do
                a = attall[here.d, :, head * HEAD_DIM : (head + 1) * HEAD_DIM].astype(F32)
                total[g, pl.ds(j * ROWS, ROWS)] = jnp.broadcast_to(
                    jnp.sum(a * do.astype(F32), axis=1, keepdims=True), (ROWS, 128)
                )
            qt_s[g] = q_s[pl.ds(2 * g, 2)].reshape(2 * ROWS, HEAD_DIM).T
        oacc[...] = jnp.zeros(oacc.shape, F32)

    def write_grad_queries():
        for g in range(4):
            value = (oacc[g] * SCALE).astype(BF16)
            for j in range(2):
                head = 2 * g + j
                dq_ref[:, head * HEAD_DIM : (head + 1) * HEAD_DIM] = value[j * ROWS : (j + 1) * ROWS]

    def write_grad_keys_values():
        d_red.final(d_final)
        dk_ref[...] = d_final[0]
        dv_ref[...] = d_final[1]

    def wait_w():
        for j in range(8):
            load_w(j).wait()

    def hand():
        handed(0).start()
        handed(1).start()

    def take():
        taken(0)
        taken(1)

    def clear():
        gacc[...] = jnp.zeros(gacc.shape, F32)

    def summed(*order):
        for r in order:
            sib_sum(r).wait_recv()

    def write_grad_weight():
        gw_ref[...] = gacc[...].astype(BF16)

    def drain():
        for group in (kvg, kvsib, gg, ag, sib, cg, c_red, d_red):
            group.drain()
        for i in range(2):
            handed(i).wait_send()
        for r in range(4):
            sib_sum(r).wait_send()

    steps = [
        (kvg.pair,),
        (gg.start_pair,),
        (kvg.near,),
        (kvsib.start, 1),
        (kvsib.start, 2, 3),
        (kvg.near_pair,),
        (kvsib.start, 4, 5),
        (hand,),
        (kvsib.got, 2, 4),
        (kvsib.got, 3, 5),
        (maxima, zd),
        (wait_w,),
        (kvsib.got, 0, 1),
        (gg.near,),
        (head_grads, yu, h),
        (kvg.far,),
        (kvsib.start, 6),
        (head_grads, yd, h),
        (kvg.far_pair,),
        (maxima, zu),
        (kvsib.start, 7),
        (take,),
        (gg.pair,),
        (head_grads, here.y, o),
        (kvsib.got, 6, 7),
        (maxima, zf),
        (maxima, here.z),
        (cg.start_near,),
        (gg.far,),
        (spread,),
        (gg.near_over,),
        (attend, zu),
        (gg.near_pair,),
        (attend, zd),
        (attend, zf),
        (attend, here.z),
        (finish_attention,),
        (c_red.far_up,),
        (ag.start_pair,),
        (c_red.far_dn,),
        (head_grads, yd, o),
        (ag.start_near,),
        (head_grads, yu, o),
        (head_grads, yf, h),
        (gg.far_pair,),
        (cg.start_pair,),
        (head_grads, yf, o),
        (c_red.near_up,),
        (clear,),
        (head_grads, here.y, h),
        (c_red.near_dn,),
        (prepare_backward,),
        (c_red.comb_dn,),
        (ag.near,),
        (plane_a, 0, zf),
        (ag.pair,),
        (c_red.comb_up,),
        (sib.start, 0),
        (plane_b, 0, zf),
        (plane_a, 1, zd),
        (plane_b, 1, zd),
        (ag.far,),
        (plane_a, 2, zu),
        (plane_b, 2, zu),
        (cg.near,),
        (summed, 0),
        (ag.near_pair,),
        (plane_a, 3, here.z),
        (sib.start, 6),
        (d_red.far,),
        (sib.start, 4, 5),
        (cg.pair,),
        (sib.start, 2, 3),
        (summed, 2),
        (c_red.pair,),
        (cg.near_over,),
        (sib.start, 1),
        (plane_b, 3, here.z),
        (cg.far,),
        (ag.far_pair,),
        (sib.start, 7),
        (write_grad_queries,),
        (summed, 1),
        (d_red.near,),
        (d_red.comb,),
        (summed, 3),
        (sib.got, 0, 1, 2, 3, 4, 5, 6, 7),
        (weight_part, here.y, h),
        (weight_part, yf, h),
        (weight_part, yd, h),
        (weight_part, here.y, o),
        (cg.near_pair,),
        (weight_part, yu, o),
        (d_red.pair,),
        (weight_part, yu, h),
        (write_grad_keys_values,),
        (c_red.final, out_ref),
        (weight_part, yd, o),
        (cg.far_pair,),
        (weight_part, yf, o),
        (write_grad_weight,),
        (drain,),
    ]
    for step, *given in steps:
        step(*given)


def vmem():
    return pl.BlockSpec(memory_space=pltpu.VMEM)


def smem():
    return pl.BlockSpec(memory_space=pltpu.SMEM)


def anywhere():
    return pl.BlockSpec(memory_space=pl.ANY)


def dma(n):
    return pltpu.SemaphoreType.DMA((n,))


def result_shapes():
    shape = jax.ShapeDtypeStruct
    return (
        shape((ROWS, COLS), BF16),
        shape((ROWS, COLS), BF16),
        shape((ROWS, HEAD_DIM), BF16),
        shape((ROWS, HEAD_DIM), BF16),
        shape((COLS, COLS // 2), BF16),
    )


def layer(q, k, v, w, g, place, length):
    return pl.pallas_call(
        layer_kernel,
        out_shape=result_shapes(),
        in_specs=[vmem(), vmem(), vmem(), anywhere(), vmem(), smem(), smem()],
        out_specs=(vmem(),) * 5,
        scratch_shapes=[
            pltpu.VMEM((2, 16, ROWS, HEAD_DIM), BF16),
            pltpu.VMEM((8, ROWS, COLS), BF16),
            pltpu.VMEM((8, COLS, COLS), BF16),
            pltpu.VMEM((16, ROWS, COLS), BF16),
            pltpu.VMEM((8, 2 * ROWS, COLS // 2), BF16),
            pltpu.VMEM((GROUP, ROWS, HEAD_DIM), BF16),
            pltpu.VMEM((GROUP, ROWS, HEAD_DIM), BF16),
            pltpu.VMEM((4, HEAD_DIM, 2 * ROWS), BF16),
            pltpu.VMEM((4, HEAD_DIM, 2 * ROWS), BF16),
            pltpu.VMEM((4, ROWS, ZK), F32),
            pltpu.VMEM((4, 2 * ROWS, 128), F32),
            pltpu.VMEM((4, 2 * ROWS, 128), F32),
            pltpu.VMEM((4, 2 * ROWS, 128), F32),
            pltpu.VMEM((COLS, ROWS), F32),
            pltpu.VMEM((HEAD_DIM, ZK), F32),
            pltpu.VMEM((HEAD_DIM, ZK), F32),
            pltpu.VMEM((4, 2, 2, ROWS, HEAD_DIM), F32),
            pltpu.VMEM((4, 2, 2, ROWS, HEAD_DIM), BF16),
            pltpu.VMEM((4, 2, 2, ROWS, HEAD_DIM), BF16),
            pltpu.VMEM((7, ROWS, COLS), BF16),
            pltpu.VMEM((7, ROWS, COLS), BF16),
            pltpu.VMEM((7, 2, ROWS, HEAD_DIM), BF16),
            pltpu.VMEM((7, 2, ROWS, HEAD_DIM), BF16),
            pltpu.VMEM((2, ROWS, HEAD_DIM), BF16),
            pltpu.VMEM((COLS, COLS // 2), F32),
            dma(8), dma(9), dma(9), dma(8), dma(8), dma(12), dma(12), dma(2), dma(2),
            dma(9), dma(9), dma(8), dma(8), dma(12), dma(12), dma(7), dma(7), dma(4), dma(4),
            dma(7), dma(7),
        ],
        compiler_params=pltpu.CompilerParams(
            collective_id=0, has_side_effects=True, vmem_limit_bytes=63 * 2**20
        ),
        cost_estimate=pl.CostEstimate(flops=24 * 10**9, bytes_accessed=24 * 10**6, transcendentals=12 * 10**6),
    )(q, k, v, w, g, place, length)


def hand_over_kernel(*refs):
    for source, result in zip(refs[:5], refs[5:]):
        result[...] = source[...]


def hand_over(*arrays):
    return pl.pallas_call(
        hand_over_kernel,
        out_shape=result_shapes(),
        in_specs=[vmem()] * 5,
        out_specs=(vmem(),) * 5,
    )(*arrays)


def on_device(q, k, v, w, g, place, length):
    return hand_over(*layer(q, k, v, w, g, place, length))


def solution(mesh):
    in_specs = (P("dc", "tp"), P("dc", "tp"), P("dc", "tp"), P("tp", None), P("dc", "tp"), P(), P())
    out_specs = (P("dc", "tp"), P("dc", "tp"), P("dc", "tp"), P("dc", "tp"), P("tp", "dc"))
    return jax.shard_map(
        on_device, mesh=mesh, in_specs=in_specs, out_specs=out_specs, check_vma=False
    )
```
